512 devices in a mesh: wide: 128 (over y, z, x_hi), narrow: 4 (over x_lo, core).
Axes of the slice: x: 4 (x_hi: 2, x_lo: 2; x = x_hi * 2 + x_lo), y: 4, z: 16, core: 2. Of those that a mesh axis runs over, the one named last changes fastest.
Arguments:
- cells: bfloat16 [524288, 512], P(('wide', 'narrow')), may hold values from -700 to 700
- plate_id: int32 [524288], P(('wide', 'narrow')), may hold values from 0 to 127, as said below
- control: int32 [524288], P(('wide', 'narrow')), may hold values from 0 to 1, as said below
Outputs:
- sphered: bfloat16 [524288, 512], P(('wide', 'narrow'))
The draws below stay inside these ranges and needn't reach their ends.
Inputs may be any that keep to these rules, and one draw needn't show every extreme that they name: `plate_id`: ids never fall; plate p begins at row p * 4096 + r_p with r_0 = 0 and 1024 <= r_p < 3072 for p >= 1, both ends reached by some plate. `control`: each aligned block of 1024 rows (the rows of one device) holds exactly 93 controls.
All inputs are finite; a program needn't handle non-finite values.
Results may differ from the reference program's by a relative error of at most 0.0071.
Values may be sent and summed in bfloat16 or wider, within the bound.
No kernel may reach another device: no remote copies, remote signals or barrier semaphores. Data moves between devices by JAX's collectives and lax.ppermute only.
A program may use at most 64 MiB of HBM per device.

```python
import math
import jax
import jax.numpy as jnp
from jax import lax

F = 512
ROWS_DEV = 1024
ITERS = 4
CTRL_DEV = 93
GROUP = 4096
PLATES = 128
CELLS = 524288


def draw_cells(key, part):
    key = jax.random.fold_in(key, 11)
    scales = jnp.exp(jax.random.uniform(jax.random.fold_in(key, 1), (F,), jnp.float32, 0.0, math.log(10.0)))
    shifts = jax.random.uniform(jax.random.fold_in(key, 2), (F,), jnp.float32, -3.0, 3.0) * scales
    loading = jax.random.truncated_normal(jax.random.fold_in(key, 3), -5.0, 5.0, (CELLS, 1), jnp.float32)
    noise = jax.random.truncated_normal(jax.random.fold_in(key, 4), -5.0, 5.0, (CELLS, F), jnp.float32)
    pattern = 0.5 * jax.random.truncated_normal(jax.random.fold_in(key, 5), -5.0, 5.0, (1, F), jnp.float32)
    row_scale = jnp.ones((CELLS, 1), jnp.float32)
    values = scales[None, :] * row_scale * (noise + loading * pattern) + shifts[None, :]
    return values.astype(jnp.bfloat16)


def draw_plate_id(key, part):
    key = jax.random.fold_in(key, 23)
    offsets = GROUP // 4 + jax.random.randint(jax.random.fold_in(key, 1), (PLATES,), 0, GROUP // 2)
    lowest = jax.random.randint(jax.random.fold_in(key, 2), (), 1, PLATES)
    highest = 1 + lowest % (PLATES - 1)
    plate_index = jnp.arange(PLATES, dtype=jnp.int32)
    offsets = jnp.where(plate_index == lowest, GROUP // 4, offsets)
    offsets = jnp.where(plate_index == highest, 3 * GROUP // 4 - 1, offsets)
    offsets = jnp.where(plate_index == 0, 0, offsets)
    starts = (plate_index * GROUP + offsets).astype(jnp.int32)
    positions = jnp.arange(CELLS, dtype=jnp.int32)
    return (jnp.searchsorted(starts, positions, side='right') - 1).astype(jnp.int32)


def draw_control(key, part):
    key = jax.random.fold_in(key, 37)
    blocks = CELLS // ROWS_DEV
    scores = jax.random.randint(key, (blocks, ROWS_DEV), 0, 4096).astype(jnp.int32)
    scores = scores * ROWS_DEV + jnp.arange(ROWS_DEV, dtype=jnp.int32)[None, :]
    order = jnp.argsort(scores, axis=1, stable=True)
    ranks = jnp.argsort(order, axis=1, stable=True)
    return (ranks < CTRL_DEV).astype(jnp.int32).reshape(CELLS)


def setup_inputs(seed: int = 0) -> dict:
    seeds = jax.random.split(jax.random.key(seed), 4)
    cells = draw_cells(jax.random.fold_in(seeds[3], 71), 0)
    plate_id = draw_plate_id(jax.random.fold_in(seeds[3], 71), 0)
    control = draw_control(jax.random.fold_in(seeds[3], 71), 0)
    return dict(cells=cells, plate_id=plate_id, control=control)


shrink = 0.1
epsilon = 1e-05

def plate_statistics(cells, plate_id, control, plate_index):
    row_start = jnp.minimum(plate_index * GROUP, CELLS - 2 * GROUP).astype(jnp.int32)
    window = lax.dynamic_slice_in_dim(cells, row_start, 2 * GROUP, 0)
    window_ids = lax.dynamic_slice_in_dim(plate_id, row_start, 2 * GROUP, 0)
    window_flags = lax.dynamic_slice_in_dim(control, row_start, 2 * GROUP, 0)
    weight = (window_ids == plate_index) & (window_flags == 1)
    picked = jnp.where(weight[:, None], window, jnp.zeros((), jnp.bfloat16))
    gram_sum = jnp.dot(picked.T, window, preferred_element_type=jnp.float32)
    column_sums = jnp.dot(weight.astype(jnp.bfloat16)[None, :], window, preferred_element_type=jnp.float32)[0]
    control_count = jnp.sum(weight.astype(jnp.float32))
    return (gram_sum, column_sums, control_count)

def sphere_matrix(gram_sum, column_sums, control_count):
    centre = column_sums / control_count
    covariance = gram_sum / control_count - centre[:, None] * centre[None, :]
    identity = jnp.eye(F, dtype=jnp.float32)
    trace_sum = jnp.sum(jnp.diagonal(covariance))
    shrunk = (1.0 - shrink) * covariance + (shrink * trace_sum / F + epsilon) * identity
    norm_scale = jnp.sqrt(jnp.sum(shrunk * shrunk))
    iterate = shrunk / norm_scale
    inverse = identity
    for iteration in range(ITERS):
        newton_step = 1.5 * identity - 0.5 * jnp.dot(inverse, iterate, precision=lax.Precision.HIGHEST)
        iterate = jnp.dot(newton_step, iterate, precision=lax.Precision.HIGHEST)
        inverse = jnp.dot(newton_step, inverse, precision=lax.Precision.HIGHEST)
    sphere = (inverse / jnp.sqrt(norm_scale)).astype(jnp.bfloat16)
    return (sphere, centre.astype(jnp.bfloat16))

def reference(cells, plate_id, control):

    def one_plate(plate_index):
        gram_sum, column_sums, control_count = plate_statistics(cells, plate_id, control, plate_index)
        return sphere_matrix(gram_sum, column_sums, control_count)
    spheres, centres = lax.map(one_plate, jnp.arange(PLATES, dtype=jnp.int32))

    def one_group(group_index):
        row_start = (group_index * GROUP).astype(jnp.int32)
        block = lax.dynamic_slice_in_dim(cells, row_start, GROUP, 0)
        block_ids = lax.dynamic_slice_in_dim(plate_id, row_start, GROUP, 0)
        earlier = jnp.maximum(group_index - 1, 0)
        own_sphere = spheres[group_index]
        prior_sphere = spheres[earlier]
        own_term = jnp.dot(block, own_sphere, preferred_element_type=jnp.float32) - jnp.dot(centres[group_index][None, :], own_sphere, preferred_element_type=jnp.float32)
        prior_term = jnp.dot(block, prior_sphere, preferred_element_type=jnp.float32) - jnp.dot(centres[earlier][None, :], prior_sphere, preferred_element_type=jnp.float32)
        return jnp.where((block_ids == group_index)[:, None], own_term, prior_term).astype(jnp.bfloat16)
    grouped = lax.map(one_group, jnp.arange(PLATES, dtype=jnp.int32))
    return grouped.reshape(CELLS, F)
```

```python
import jax
import jax.numpy as jnp
from jax import lax
from jax.experimental import pallas as pl
from jax.experimental.pallas import tpu as pltpu
from jax.sharding import Mesh
from jax.sharding import PartitionSpec as P

ROWS = 1024
F = 512
CONTROLS = 93
BLOCK = 96
LANES = 128
SUBROWS = ROWS // LANES
MEMBERS = 4
GROUPS = 128
PACK = F + 16

shrink = 0.1
epsilon = 1e-05
f32 = jnp.float32
bf16 = jnp.bfloat16
VMEM_LIMIT = 48 * 1024 * 1024


def matmul(left, right):
    return jnp.dot(left, right, preferred_element_type=f32)


def matmul_tn(left, right):
    return lax.dot_general(left, right, (((0,), (0,)), ((), ())), preferred_element_type=f32)


def pick_kernel(cells_hbm, plate_ref, control_ref, out_ref, cells, sems):
    chunk = ROWS // 4
    copies = [
        pltpu.make_async_copy(
            cells_hbm.at[pl.ds(part * chunk, chunk)], cells.at[pl.ds(part * chunk, chunk)], sems.at[part]
        )
        for part in range(4)
    ]
    for copy in copies:
        copy.start()
    group = lax.axis_index("d") // MEMBERS
    is_control = control_ref[...] == 1
    flags = is_control.astype(f32)
    upper = lax.broadcasted_iota(jnp.int32, (LANES, LANES), 0) <= lax.broadcasted_iota(
        jnp.int32, (LANES, LANES), 1
    )
    inclusive = matmul(flags.astype(bf16), upper.astype(f32).astype(bf16))
    total = jnp.broadcast_to(jnp.sum(flags, axis=1, keepdims=True), (SUBROWS, LANES))
    sub = lax.broadcasted_iota(jnp.int32, (SUBROWS, LANES), 0)
    running = total
    for step in (1, 2, 4):
        running = running + jnp.where(sub >= step, pltpu.roll(running, step, 0), 0.0)
    rank = jnp.where(is_control, inclusive + (running - total) - 1.0, -1.0).astype(jnp.int32)
    slots = lax.broadcasted_iota(jnp.int32, (BLOCK, LANES), 0)
    chosen = jnp.concatenate(
        [
            jnp.where(slots == jnp.broadcast_to(rank[k : k + 1, :], (BLOCK, LANES)), 1.0, 0.0).astype(bf16)
            for k in range(SUBROWS)
        ],
        axis=1,
    )
    earlier = jnp.sum(jnp.where(is_control & (plate_ref[...] < group), 1.0, 0.0), keepdims=True)
    picked = None
    for part, copy in enumerate(copies):
        copy.wait()
        span = slice(part * chunk, (part + 1) * chunk)
        term = matmul(chosen[:, span], cells[span, :])
        picked = term if picked is None else picked + term
    last = lax.broadcasted_iota(jnp.int32, (BLOCK, F), 0) == BLOCK - 1
    out_ref[...] = jnp.where(last, jnp.broadcast_to(earlier, (BLOCK, F)), picked).astype(bf16)


def sphere_kernel(rows_ref, out_ref):
    index = lax.axis_index("d")
    last_home = (index // MEMBERS == GROUPS - 1) & (index % 2 == 1)
    slot = lax.broadcasted_iota(jnp.int32, (BLOCK, F), 0).astype(f32)
    blocks = []
    count = jnp.zeros((1, 1), f32)
    for block in range(2 * MEMBERS):
        values = rows_ref[block * BLOCK : (block + 1) * BLOCK, :].astype(f32)
        earlier = values[BLOCK - 1 : BLOCK, 0:1]
        if block < MEMBERS:
            keep = (slot >= earlier) & (slot < float(CONTROLS))
            count = count + (float(CONTROLS) - earlier)
        else:
            earlier = jnp.where(last_home, 0.0, earlier)
            keep = slot < earlier
            count = count + earlier
        blocks.append(jnp.where(keep, values, 0.0).astype(bf16))
    picked = jnp.concatenate(blocks, axis=0)
    scale = 1.0 / jnp.maximum(count, 1.0)
    centre_row = matmul(jnp.ones((16, 2 * MEMBERS * BLOCK), bf16), picked)[0:1, :] * scale
    centre_column = matmul_tn(picked, jnp.ones((2 * MEMBERS * BLOCK, LANES), bf16))[:, 0:1] * scale
    gram = matmul_tn(picked, picked)
    covariance = gram * scale - centre_column * centre_row
    diagonal = lax.broadcasted_iota(jnp.int32, (F, F), 0) == lax.broadcasted_iota(jnp.int32, (F, F), 1)
    trace = jnp.sum(jnp.where(diagonal, covariance, 0.0), keepdims=True)
    ridge = shrink * trace / F + epsilon
    shrunk = (1.0 - shrink) * covariance + jnp.where(diagonal, ridge, 0.0)
    norm_scale = jnp.sqrt(jnp.sum(shrunk * shrunk, keepdims=True))
    start = shrunk * (1.0 / norm_scale)
    start_b = start.astype(bf16)
    square = matmul(start_b, start_b)
    iterate = 1.5 * start - 0.5 * square
    product = matmul((0.25 * square - 1.5 * start).astype(bf16), iterate.astype(bf16))
    rest = -0.75 * start - 0.5 * (2.25 * iterate + product)
    z = 2.25
    for step in range(2):
        rest_b = rest.astype(bf16)
        square = matmul(rest_b, rest_b)
        iterate = z * start + matmul(start_b, rest_b)
        product = z * z * iterate + matmul((2.0 * z * rest + square).astype(bf16), iterate.astype(bf16))
        rest = 1.5 * rest - 0.5 * product
        z = 1.5 * z
    inverse = rest + jnp.where(diagonal, z, 0.0)
    out_ref[0:F, :] = (inverse * (1.0 / jnp.sqrt(norm_scale))).astype(bf16)
    out_ref[F:PACK, :] = jnp.broadcast_to(centre_row, (PACK - F, F)).astype(bf16)


def apply_kernel(cells_ref, plate_ref, spheres_ref, out_hbm, out, sems):
    group = lax.axis_index("d") // MEMBERS
    earlier = jnp.sum(jnp.where(plate_ref[...] < group, 1.0, 0.0), keepdims=True)
    offsets = [
        matmul(spheres_ref[s * PACK + F : (s + 1) * PACK, :], spheres_ref[s * PACK : s * PACK + F, :])[0:1, :]
        for s in range(2)
    ]
    chunk = ROWS // 4
    copies = []
    for part in range(4):
        rows = cells_ref[part * chunk : (part + 1) * chunk, :]
        index = lax.broadcasted_iota(jnp.int32, (chunk, F), 0).astype(f32) + float(part * chunk)
        before = matmul(rows, spheres_ref[0:F, :]) - offsets[0]
        own = matmul(rows, spheres_ref[PACK : PACK + F, :]) - offsets[1]
        out[part * chunk : (part + 1) * chunk, :] = jnp.where(index < earlier, before, own).astype(bf16)
        copy = pltpu.make_async_copy(
            out.at[pl.ds(part * chunk, chunk)], out_hbm.at[pl.ds(part * chunk, chunk)], sems.at[part]
        )
        copy.start()
        copies.append(copy)
    for copy in copies:
        copy.wait()


def pairs(kind):
    if kind == "chip":
        return [[2 * i, 2 * i + 1] for i in range(GROUPS * MEMBERS // 2)]
    near = [[4 * p + 3, 4 * p + 4] for p in range(GROUPS - 1)]
    far = [[4 * p + 1, 4 * p + 6] for p in range(GROUPS - 1)]
    return near + far + [[0, 2], [4 * GROUPS - 3, 4 * GROUPS - 1]]


def shards(cells, plate_id, control):
    vmem = pl.BlockSpec(memory_space=pltpu.VMEM)
    hbm = pl.BlockSpec(memory_space=pl.ANY)
    params = pltpu.CompilerParams(vmem_limit_bytes=VMEM_LIMIT)
    plates = plate_id.reshape(SUBROWS, LANES)
    block = pl.pallas_call(
        pick_kernel,
        out_shape=jax.ShapeDtypeStruct((BLOCK, F), bf16),
        in_specs=[hbm, vmem, vmem],
        out_specs=vmem,
        scratch_shapes=[pltpu.VMEM((ROWS, F), bf16), pltpu.SemaphoreType.DMA((4,))],
        compiler_params=params,
        name="pick_controls",
    )(cells, plates, control.reshape(SUBROWS, LANES))
    members = [[MEMBERS * g + m for m in range(MEMBERS)] for g in range(GROUPS)]
    group_rows = lax.all_gather(block, "d", axis_index_groups=members, tiled=True)
    plate_rows = lax.all_gather(group_rows, "d", axis_index_groups=pairs("plate"), tiled=True)
    sphere = pl.pallas_call(
        sphere_kernel,
        out_shape=jax.ShapeDtypeStruct((PACK, F), bf16),
        in_specs=[vmem],
        out_specs=vmem,
        scratch_shapes=[],
        compiler_params=params,
        name="sphere",
    )(plate_rows)
    spheres = lax.all_gather(sphere, "d", axis_index_groups=pairs("chip"), tiled=True)
    return pl.pallas_call(
        apply_kernel,
        out_shape=jax.ShapeDtypeStruct((ROWS, F), bf16),
        in_specs=[vmem, vmem, vmem],
        out_specs=hbm,
        scratch_shapes=[pltpu.VMEM((ROWS, F), bf16), pltpu.SemaphoreType.DMA((4,))],
        compiler_params=params,
        name="apply_spheres",
    )(cells, plates, spheres)


def solution(mesh):
    line = Mesh(mesh.devices.reshape(-1), ("d",))
    return jax.shard_map(
        shards,
        mesh=line,
        in_specs=(P("d", None), P("d"), P("d")),
        out_specs=P("d", None),
        check_vma=False,
    )
```

```python
import jax
import jax.numpy as jnp
from jax import lax
from jax.experimental import pallas as pl
from jax.experimental.pallas import tpu as pltpu
from jax.sharding import Mesh
from jax.sharding import PartitionSpec as P

ROWS = 1024
F = 512
CONTROLS = 93
BLOCK = 96
LANES = 128
SUBROWS = ROWS // LANES
MEMBERS = 4
CHUNKS = 4
HOME = 3 * BLOCK
GROUPS = 128
HALF = F // 2
CENTRE = HALF + HALF // 2
PACK = CENTRE + 16

shrink = 0.1
epsilon = 1e-05
f32 = jnp.float32
bf16 = jnp.bfloat16
VMEM_LIMIT = 48 * 1024 * 1024


def matmul(left, right):
    return jnp.dot(left, right, preferred_element_type=f32)


def matmul_tn(left, right):
    return lax.dot_general(left, right, (((0,), (0,)), ((), ())), preferred_element_type=f32)


def pick_kernel(cells_hbm, plate_hbm, control_hbm, out_ref, cells, plate_ref, control_ref, sems, flag_sems):
    chunk = ROWS // 4
    flag_copies = [
        pltpu.make_async_copy(control_hbm, control_ref, flag_sems.at[0]),
        pltpu.make_async_copy(plate_hbm, plate_ref, flag_sems.at[1]),
    ]
    copies = [
        pltpu.make_async_copy(
            cells_hbm.at[pl.ds(part * chunk, chunk)], cells.at[pl.ds(part * chunk, chunk)], sems.at[part]
        )
        for part in range(4)
    ]
    for copy in flag_copies + copies:
        copy.start()
    group = lax.axis_index("d") // MEMBERS
    for copy in flag_copies:
        copy.wait()
    is_control = control_ref[...] == 1
    flags = is_control.astype(f32)
    upper = lax.broadcasted_iota(jnp.int32, (LANES, LANES), 0) <= lax.broadcasted_iota(
        jnp.int32, (LANES, LANES), 1
    )
    inclusive = matmul(flags.astype(bf16), upper.astype(f32).astype(bf16))
    total = jnp.broadcast_to(jnp.sum(flags, axis=1, keepdims=True), (SUBROWS, LANES))
    sub = lax.broadcasted_iota(jnp.int32, (SUBROWS, LANES), 0)
    running = total
    for step in (1, 2, 4):
        running = running + jnp.where(sub >= step, pltpu.roll(running, step, 0), 0.0)
    rank = jnp.where(is_control, inclusive + (running - total) - 1.0, -1.0).astype(jnp.int32)
    slots = lax.broadcasted_iota(jnp.int32, (BLOCK, LANES), 0)
    chosen = jnp.concatenate(
        [
            jnp.where(slots == jnp.broadcast_to(rank[k : k + 1, :], (BLOCK, LANES)), 1.0, 0.0).astype(bf16)
            for k in range(SUBROWS)
        ],
        axis=1,
    )
    earlier = jnp.sum(jnp.where(is_control & (plate_ref[...] < group), 1.0, 0.0), keepdims=True)
    picked = None
    for part, copy in enumerate(copies):
        copy.wait()
        span = slice(part * chunk, (part + 1) * chunk)
        term = matmul(chosen[:, span], cells[span, :])
        picked = term if picked is None else picked + term
    last = lax.broadcasted_iota(jnp.int32, (BLOCK, F), 0) == BLOCK - 1
    out_ref[...] = jnp.where(last, jnp.broadcast_to(earlier, (BLOCK, F)), picked).astype(bf16)


def sphere_kernel(rows_ref, group_ref, first_ref, out_ref, start_ref, rest_ref, start_b, rest_b, left_b, iterate_b):
    index = lax.axis_index("d")
    group = index // MEMBERS
    home = (group + index) % 2
    last_home = (group == GROUPS - 1) & (home == 1)
    first_plate = group + home == 1
    slot = lax.broadcasted_iota(jnp.int32, (BLOCK, F), 0).astype(f32)
    blocks = []
    count = jnp.zeros((1, 1), f32)
    for block in range(6):
        values = rows_ref[block * BLOCK : (block + 1) * BLOCK, :].astype(f32)
        earlier = values[BLOCK - 1 : BLOCK, 0:1]
        if block < 3:
            keep = (slot >= earlier) & (slot < float(CONTROLS))
            count = count + (float(CONTROLS) - earlier)
        else:
            earlier = jnp.where(last_home, 0.0, earlier)
            keep = slot < earlier
            count = count + earlier
        blocks.append(jnp.where(keep, values, 0.0).astype(bf16))
    opening = jnp.where(group == 0, group_ref[...].astype(f32), first_ref[...].astype(f32))
    blocks.append(jnp.where(first_plate & (slot < float(CONTROLS)), opening, 0.0).astype(bf16))
    count = count + jnp.where(first_plate, float(CONTROLS), 0.0)
    picked = jnp.concatenate(blocks, axis=0)
    scale = 1.0 / jnp.maximum(count, 1.0)
    centre_row = matmul(jnp.ones((16, 7 * BLOCK), bf16), picked)[0:1, :] * scale
    centre_column = matmul_tn(picked, jnp.ones((7 * BLOCK, LANES), bf16))[:, 0:1] * scale
    gram = matmul_tn(picked, picked)
    covariance = gram * scale - centre_column * centre_row
    diagonal = lax.broadcasted_iota(jnp.int32, (F, F), 0) == lax.broadcasted_iota(jnp.int32, (F, F), 1)
    trace = jnp.sum(jnp.where(diagonal, covariance, 0.0), keepdims=True)
    ridge = shrink * trace / F + epsilon
    shrunk = (1.0 - shrink) * covariance + jnp.where(diagonal, ridge, 0.0)
    norm_scale = jnp.sqrt(jnp.sum(shrunk * shrunk, keepdims=True))
    start = shrunk * (1.0 / norm_scale)
    start_ref[...] = start
    start_b[...] = start.astype(bf16)
    parts = [slice(k * HALF, (k + 1) * HALF) for k in range(2)]
    for part in parts:
        a = start_ref[part, :]
        square = matmul(start_b[part, :], start_b[...])
        iterate = 1.5 * a - 0.5 * square
        left_b[part, :] = (0.25 * square - 1.5 * a).astype(bf16)
        iterate_b[part, :] = iterate.astype(bf16)
        rest_ref[part, :] = -0.75 * a - 1.125 * iterate
    z = 2.25
    for step in range(2):
        for part in parts:
            rest = rest_ref[part, :] - 0.5 * matmul(left_b[part, :], iterate_b[...])
            rest_ref[part, :] = rest
            rest_b[part, :] = rest.astype(bf16)
        for part in parts:
            rest = rest_ref[part, :]
            square = matmul(rest_b[part, :], rest_b[...])
            iterate = z * start_ref[part, :] + matmul(start_b[part, :], rest_b[...])
            left_b[part, :] = (2.0 * z * rest + square).astype(bf16)
            iterate_b[part, :] = iterate.astype(bf16)
            rest_ref[part, :] = 1.5 * rest - (0.5 * z * z) * iterate
        z = 1.5 * z
    rest = jnp.concatenate([rest_ref[part, :] - 0.5 * matmul(left_b[part, :], iterate_b[...]) for part in parts], axis=0)
    inverse = rest + jnp.where(diagonal, z, 0.0)
    sphere = (inverse * (1.0 / jnp.sqrt(norm_scale))).astype(bf16)
    out_ref[0:HALF, :] = sphere[0:HALF, :]
    out_ref[HALF:CENTRE, 0:HALF] = sphere[HALF : HALF + HALF // 2, HALF:F]
    out_ref[HALF:CENTRE, HALF:F] = sphere[HALF + HALF // 2 : F, HALF:F]
    out_ref[CENTRE:PACK, :] = jnp.broadcast_to(centre_row, (PACK - CENTRE, F)).astype(bf16)


def apply_kernel(cells_ref, plate_ref, packed_ref, out_hbm, out, spheres, sems):
    group = lax.axis_index("d") // MEMBERS
    parity = group % 2
    earlier = jnp.sum(jnp.where(plate_ref[...] < group, 1, 0))
    offsets = []
    for side, core in enumerate((parity, 1 - parity)):
        upper = packed_ref[core, 0:HALF, :]
        spheres[side, 0:HALF, :] = upper
        spheres[side, HALF:F, 0:HALF] = upper[:, HALF:F].T
        spheres[side, HALF:CENTRE, HALF:F] = packed_ref[core, HALF:CENTRE, 0:HALF]
        spheres[side, CENTRE:F, HALF:F] = packed_ref[core, HALF:CENTRE, HALF:F]
        offsets.append(matmul(packed_ref[core, CENTRE:PACK, :], spheres[side])[0:1, :])
    chunk = ROWS // CHUNKS
    copies = []
    for part in range(CHUNKS):
        start = part * chunk
        span = slice(start, start + chunk)
        side = jnp.where(earlier > start, 0, 1)
        offset = jnp.where(earlier > start, offsets[0], offsets[1])
        out[span, :] = (matmul(cells_ref[span, :], spheres[side]) - offset).astype(bf16)

        @pl.when((earlier > start) & (earlier < start + chunk))
        def _(start=start, span=span):
            index = lax.broadcasted_iota(jnp.int32, (chunk, F), 0) + start
            own = matmul(cells_ref[span, :], spheres[1]) - offsets[1]
            out[span, :] = jnp.where(index < earlier, out[span, :].astype(f32), own).astype(bf16)

        copy = pltpu.make_async_copy(out.at[pl.ds(start, chunk)], out_hbm.at[pl.ds(start, chunk)], sems.at[part])
        copy.start()
        copies.append(copy)
    for copy in copies:
        copy.wait()


def pairs(kind):
    if kind == "chip":
        return [[2 * i, 2 * i + 1] for i in range(GROUPS * MEMBERS // 2)]
    first = [MEMBERS * p + 1 - p % 2 for p in range(GROUPS)]
    near = [[d + 2, d + 4] for d in first[:-1]]
    far = [[d, d + 6] for d in first[:-1]]
    return near + far + [[0, 2], [first[-1], first[-1] + 2]]


def shards(cells, plate_id, control):
    vmem = pl.BlockSpec(memory_space=pltpu.VMEM)
    hbm = pl.BlockSpec(memory_space=pltpu.HBM)
    params = pltpu.CompilerParams(vmem_limit_bytes=VMEM_LIMIT)
    plates = plate_id.reshape(SUBROWS, LANES)
    block = pl.pallas_call(
        pick_kernel,
        out_shape=jax.ShapeDtypeStruct((BLOCK, F), bf16),
        in_specs=[hbm, hbm, hbm],
        out_specs=vmem,
        scratch_shapes=[
            pltpu.VMEM((ROWS, F), bf16),
            pltpu.VMEM((SUBROWS, LANES), jnp.int32),
            pltpu.VMEM((SUBROWS, LANES), jnp.int32),
            pltpu.SemaphoreType.DMA((4,)),
            pltpu.SemaphoreType.DMA((2,)),
        ],
        name="pick_controls",
    )(cells, plates, control.reshape(SUBROWS, LANES))
    members = [[MEMBERS * g + m for m in range(MEMBERS)] for g in range(GROUPS)]
    group_rows = lax.all_gather(block, "d", axis_index_groups=members, tiled=True)
    index = lax.axis_index("d")
    home = lax.rem(index // MEMBERS + index, 2)
    side = lax.dynamic_slice_in_dim(group_rows, home * BLOCK, HOME, 0)
    opening = group_rows[0:BLOCK]
    first = lax.ppermute(opening, "d", [(0, 5), (2, 7)])
    plate_rows = lax.all_gather(side, "d", axis_index_groups=pairs("plate"), tiled=True)
    sphere = pl.pallas_call(
        sphere_kernel,
        out_shape=jax.ShapeDtypeStruct((PACK, F), bf16),
        in_specs=[vmem, vmem, vmem],
        out_specs=vmem,
        scratch_shapes=[pltpu.VMEM((F, F), f32)] * 2 + [pltpu.VMEM((F, F), bf16)] * 4,
        compiler_params=params,
        name="sphere",
    )(plate_rows, opening, first)
    spheres = lax.all_gather(sphere, "d", axis_index_groups=pairs("chip"), tiled=True)
    return pl.pallas_call(
        apply_kernel,
        out_shape=jax.ShapeDtypeStruct((ROWS, F), bf16),
        in_specs=[vmem, vmem, vmem],
        out_specs=hbm,
        scratch_shapes=[
            pltpu.VMEM((ROWS, F), bf16),
            pltpu.VMEM((2, F, F), bf16),
            pltpu.SemaphoreType.DMA((CHUNKS,)),
        ],
        compiler_params=params,
        name="apply_spheres",
    )(cells, plates, spheres.reshape(2, PACK, F))


def solution(mesh):
    line = Mesh(mesh.devices.reshape(-1), ("d",))
    return jax.shard_map(
        shards,
        mesh=line,
        in_specs=(P("d", None), P("d"), P("d")),
        out_specs=P("d", None),
        check_vma=False,
    )
```

```python
import jax
import jax.numpy as jnp
from jax import lax
from jax.experimental import pallas as pl
from jax.experimental.pallas import tpu as pltpu
from jax.sharding import Mesh
from jax.sharding import PartitionSpec as P

ROWS = 1024
F = 512
CONTROLS = 93
BLOCK = 96
LANES = 128
SUBROWS = ROWS // LANES
MEMBERS = 4
CHUNKS = 4
HOME = 3 * BLOCK
GROUPS = 128
HALF = F // 2
CENTRE = HALF + HALF // 2
PACK = CENTRE + 16

shrink = 0.1
epsilon = 1e-05
f32 = jnp.float32
bf16 = jnp.bfloat16
VMEM_LIMIT = 48 * 1024 * 1024


def matmul(left, right):
    return jnp.dot(left, right, preferred_element_type=f32)


def matmul_tn(left, right):
    return lax.dot_general(left, right, (((0,), (0,)), ((), ())), preferred_element_type=f32)


def pick_kernel(cells_hbm, plate_hbm, control_hbm, out_ref, cells, plate_ref, control_ref, sems, flag_sems):
    chunk = ROWS // 4
    flag_copies = [
        pltpu.make_async_copy(control_hbm, control_ref, flag_sems.at[0]),
        pltpu.make_async_copy(plate_hbm, plate_ref, flag_sems.at[1]),
    ]
    copies = [
        pltpu.make_async_copy(
            cells_hbm.at[pl.ds(part * chunk, chunk)], cells.at[pl.ds(part * chunk, chunk)], sems.at[part]
        )
        for part in range(4)
    ]
    for copy in flag_copies + copies:
        copy.start()
    group = lax.axis_index("d") // MEMBERS
    for copy in flag_copies:
        copy.wait()
    is_control = control_ref[...] == 1
    flags = is_control.astype(f32)
    upper = lax.broadcasted_iota(jnp.int32, (LANES, LANES), 0) <= lax.broadcasted_iota(
        jnp.int32, (LANES, LANES), 1
    )
    inclusive = matmul(flags.astype(bf16), upper.astype(f32).astype(bf16))
    total = jnp.broadcast_to(jnp.sum(flags, axis=1, keepdims=True), (SUBROWS, LANES))
    sub = lax.broadcasted_iota(jnp.int32, (SUBROWS, LANES), 0)
    running = total
    for step in (1, 2, 4):
        running = running + jnp.where(sub >= step, pltpu.roll(running, step, 0), 0.0)
    rank = jnp.where(is_control, inclusive + (running - total) - 1.0, -1.0).astype(jnp.int32)
    slots = lax.broadcasted_iota(jnp.int32, (BLOCK, LANES), 0)
    chosen = jnp.concatenate(
        [
            jnp.where(slots == jnp.broadcast_to(rank[k : k + 1, :], (BLOCK, LANES)), 1.0, 0.0).astype(bf16)
            for k in range(SUBROWS)
        ],
        axis=1,
    )
    earlier = jnp.sum(jnp.where(is_control & (plate_ref[...] < group), 1.0, 0.0), keepdims=True)
    picked = None
    for part, copy in enumerate(copies):
        copy.wait()
        span = slice(part * chunk, (part + 1) * chunk)
        term = matmul(chosen[:, span], cells[span, :])
        picked = term if picked is None else picked + term
    last = lax.broadcasted_iota(jnp.int32, (BLOCK, F), 0) == BLOCK - 1
    out_ref[...] = jnp.where(last, jnp.broadcast_to(earlier, (BLOCK, F)), picked).astype(bf16)


def sphere_kernel(rows_ref, group_ref, first_ref, out_ref, start_ref, rest_ref, start_b, rest_b, left_b, iterate_b):
    index = lax.axis_index("d")
    group = index // MEMBERS
    home = (group + index) % 2
    last_home = (group == GROUPS - 1) & (home == 1)
    first_plate = group + home == 1
    slot = lax.broadcasted_iota(jnp.int32, (BLOCK, LANES), 0).astype(f32)
    blocks = []
    count = jnp.zeros((1, 1), f32)

    def keep(rows, low, high):
        flags = jnp.where((slot >= low) & (slot < high), 1.0, 0.0).astype(bf16)
        blocks.append(rows * jnp.concatenate([flags] * (F // LANES), axis=1))

    for block in range(6):
        earlier = rows_ref[(block + 1) * BLOCK - 16 : (block + 1) * BLOCK, 0:LANES].astype(f32)[15:16, 0:1]
        if block < 3:
            low, high = earlier, jnp.full((1, 1), float(CONTROLS), f32)
        else:
            low, high = jnp.zeros((1, 1), f32), jnp.where(last_home, 0.0, earlier)
        keep(rows_ref[block * BLOCK : (block + 1) * BLOCK, :], low, high)
        count = count + (high - low)
    opening = jnp.where(first_plate, float(CONTROLS), 0.0)
    keep(jnp.where(group == 0, group_ref[...], first_ref[...]), 0.0, opening)
    count = count + opening
    picked = jnp.concatenate(blocks, axis=0)
    scale = 1.0 / jnp.maximum(count, 1.0)
    centre_row = matmul(jnp.ones((16, 7 * BLOCK), bf16), picked)[0:1, :] * scale
    centre_column = jnp.broadcast_to(centre_row, (8, F)).T[:, 0:1]
    parts = [slice(0, HALF), slice(HALF, F)]
    quarters = [slice(k, k + LANES) for k in range(0, F, LANES)]
    eye = lax.broadcasted_iota(jnp.int32, (LANES, LANES), 0) == lax.broadcasted_iota(jnp.int32, (LANES, LANES), 1)
    squares = jnp.zeros((1, F), f32)
    for part in parts:
        covariance = matmul_tn(picked[:, part], picked) * scale - centre_column[part, :] * centre_row
        start_ref[part, :] = covariance
        squares = squares + jnp.sum(covariance * covariance, axis=0, keepdims=True)
    traces = jnp.zeros((1, LANES), f32)
    for span in quarters:
        traces = traces + jnp.sum(jnp.where(eye, start_ref[span, span], 0.0), axis=0, keepdims=True)
    trace = jnp.sum(traces, keepdims=True)
    ridge = shrink * trace / F + epsilon
    keep_part = 1.0 - shrink
    norm_square = (
        keep_part * keep_part * jnp.sum(squares, keepdims=True) + 2.0 * keep_part * ridge * trace + F * ridge * ridge
    )
    norm_scale = jnp.sqrt(norm_square)
    inverse_norm = 1.0 / norm_scale
    for part in parts:
        start_ref[part, :] = start_ref[part, :] * (keep_part * inverse_norm)
    for span in quarters:
        start_ref[span, span] = start_ref[span, span] + jnp.where(eye, ridge * inverse_norm, 0.0)
    for part in parts:
        start_b[part, :] = start_ref[part, :].astype(bf16)
    for part in parts:
        a = start_ref[part, :]
        square = matmul(start_b[part, :], start_b[...])
        iterate = 1.5 * a - 0.5 * square
        left_b[part, :] = (0.25 * square - 1.5 * a).astype(bf16)
        iterate_b[part, :] = iterate.astype(bf16)
        rest_ref[part, :] = -0.75 * a - 1.125 * iterate
    z = 2.25
    for step in range(2):
        for part in parts:
            rest = rest_ref[part, :] - 0.5 * matmul(left_b[part, :], iterate_b[...])
            rest_ref[part, :] = rest
            rest_b[part, :] = rest.astype(bf16)
        for part in parts:
            rest = rest_ref[part, :]
            both = matmul(jnp.concatenate([rest_b[part, :], start_b[part, :]], axis=0), rest_b[...])
            square = both[0:HALF, :]
            iterate = z * start_ref[part, :] + both[HALF:F, :]
            left_b[part, :] = (2.0 * z * rest + square).astype(bf16)
            iterate_b[part, :] = iterate.astype(bf16)
            rest_ref[part, :] = 1.5 * rest - (0.5 * z * z) * iterate
        z = 1.5 * z
    gain = lax.rsqrt(norm_scale)
    for span in quarters:
        rest_ref[span, span] = rest_ref[span, span] + jnp.where(eye, z, 0.0)
    upper, lower = parts
    sphere = (rest_ref[upper, :] - 0.5 * matmul(left_b[upper, :], iterate_b[...])) * gain
    out_ref[upper, :] = sphere.astype(bf16)
    corner = (rest_ref[lower, lower] - 0.5 * matmul(left_b[lower, :], iterate_b[:, lower])) * gain
    out_ref[HALF:CENTRE, 0:HALF] = corner[0 : HALF // 2, :].astype(bf16)
    out_ref[HALF:CENTRE, HALF:F] = corner[HALF // 2 : HALF, :].astype(bf16)
    out_ref[CENTRE:PACK, :] = jnp.broadcast_to(centre_row, (PACK - CENTRE, F)).astype(bf16)


def apply_kernel(cells_ref, plate_ref, packed_ref, out_hbm, out, spheres, sems):
    group = lax.axis_index("d") // MEMBERS
    parity = group % 2
    earlier = jnp.sum(jnp.where(plate_ref[...] < group, 1, 0))
    offsets = []
    for side, core in enumerate((parity, 1 - parity)):
        upper = packed_ref[core, 0:HALF, :]
        spheres[side, 0:HALF, :] = upper
        spheres[side, HALF:F, 0:HALF] = upper[:, HALF:F].T
        spheres[side, HALF:CENTRE, HALF:F] = packed_ref[core, HALF:CENTRE, 0:HALF]
        spheres[side, CENTRE:F, HALF:F] = packed_ref[core, HALF:CENTRE, HALF:F]
        offsets.append(matmul(packed_ref[core, CENTRE:PACK, :], spheres[side])[0:1, :])
    chunk = ROWS // CHUNKS
    mixed = jnp.minimum(earlier // chunk, CHUNKS - 1)
    rows = cells_ref[pl.ds(pl.multiple_of(mixed * chunk, chunk), chunk), :]
    own = matmul(rows, spheres[1]) - offsets[1]
    slot = lax.broadcasted_iota(jnp.int32, (chunk, F), 0)
    copies = []
    for part in range(CHUNKS):
        start = part * chunk
        span = slice(start, start + chunk)
        side = jnp.where(earlier > start, 0, 1)
        offset = jnp.where(earlier > start, offsets[0], offsets[1])
        values = matmul(cells_ref[span, :], spheres[side]) - offset
        limit = jnp.where(mixed == part, earlier - start, chunk)
        out[span, :] = jnp.where(slot < limit, values, own).astype(bf16)
        copy = pltpu.make_async_copy(out.at[pl.ds(start, chunk)], out_hbm.at[pl.ds(start, chunk)], sems.at[part])
        copy.start()
        copies.append(copy)
    for copy in copies:
        copy.wait()


def pairs(kind):
    if kind == "chip":
        return [[2 * i, 2 * i + 1] for i in range(GROUPS * MEMBERS // 2)]
    first = [MEMBERS * p + 1 - p % 2 for p in range(GROUPS)]
    near = [[d + 2, d + 4] for d in first[:-1]]
    far = [[d, d + 6] for d in first[:-1]]
    return near + far + [[0, 2], [first[-1], first[-1] + 2]]


def shards(cells, plate_id, control):
    vmem = pl.BlockSpec(memory_space=pltpu.VMEM)
    hbm = pl.BlockSpec(memory_space=pltpu.HBM)
    params = pltpu.CompilerParams(vmem_limit_bytes=VMEM_LIMIT)
    plates = plate_id.reshape(SUBROWS, LANES)
    block = pl.pallas_call(
        pick_kernel,
        out_shape=jax.ShapeDtypeStruct((BLOCK, F), bf16),
        in_specs=[hbm, hbm, hbm],
        out_specs=vmem,
        scratch_shapes=[
            pltpu.VMEM((ROWS, F), bf16),
            pltpu.VMEM((SUBROWS, LANES), jnp.int32),
            pltpu.VMEM((SUBROWS, LANES), jnp.int32),
            pltpu.SemaphoreType.DMA((4,)),
            pltpu.SemaphoreType.DMA((2,)),
        ],
        compiler_params=params,
        name="pick_controls",
    )(*(pltpu.with_memory_space_constraint(x, pltpu.HBM) for x in (cells, plates, control.reshape(SUBROWS, LANES))))
    members = [[MEMBERS * g + m for m in range(MEMBERS)] for g in range(GROUPS)]
    group_rows = lax.all_gather(block, "d", axis_index_groups=members, tiled=True)
    index = lax.axis_index("d")
    home = (index ^ (index >> 2)) & 1
    side = lax.dynamic_slice_in_dim(group_rows, home * BLOCK, HOME, 0)
    opening = group_rows[0:BLOCK]
    first = lax.ppermute(opening, "d", [(0, 5), (2, 7)])
    plate_rows = lax.all_gather(side, "d", axis_index_groups=pairs("plate"), tiled=True)
    sphere = pl.pallas_call(
        sphere_kernel,
        out_shape=jax.ShapeDtypeStruct((PACK, F), bf16),
        in_specs=[vmem, vmem, vmem],
        out_specs=vmem,
        scratch_shapes=[pltpu.VMEM((F, F), f32)] * 2 + [pltpu.VMEM((F, F), bf16)] * 4,
        compiler_params=params,
        name="sphere",
    )(plate_rows, opening, first)
    spheres = lax.all_gather(sphere, "d", axis_index_groups=pairs("chip"), tiled=True)
    return pl.pallas_call(
        apply_kernel,
        out_shape=jax.ShapeDtypeStruct((ROWS, F), bf16),
        in_specs=[vmem, vmem, vmem],
        out_specs=hbm,
        scratch_shapes=[
            pltpu.VMEM((ROWS, F), bf16),
            pltpu.VMEM((2, F, F), bf16),
            pltpu.SemaphoreType.DMA((CHUNKS,)),
        ],
        compiler_params=params,
        name="apply_spheres",
    )(cells, plates, spheres.reshape(2, PACK, F))


def solution(mesh):
    line = Mesh(mesh.devices.reshape(-1), ("d",))
    return jax.shard_map(
        shards,
        mesh=line,
        in_specs=(P("d", None), P("d"), P("d")),
        out_specs=P("d", None),
        check_vma=False,
    )
```

```python
import jax
import jax.numpy as jnp
from jax import lax
from jax.experimental import pallas as pl
from jax.experimental.pallas import tpu as pltpu
from jax.sharding import Mesh
from jax.sharding import PartitionSpec as P

ROWS = 1024
F = 512
CONTROLS = 93
BLOCK = 96
LANES = 128
SUBROWS = ROWS // LANES
MEMBERS = 4
CHUNKS = 8
HOME = 3 * BLOCK
GROUPS = 128
HALF = F // 2
CENTRE = HALF + HALF // 2
PACK = CENTRE + 16

shrink = 0.1
epsilon = 1e-05
f32 = jnp.float32
bf16 = jnp.bfloat16
VMEM_LIMIT = 48 * 1024 * 1024


def matmul(left, right):
    return jnp.dot(left, right, preferred_element_type=f32)


def matmul_tn(left, right):
    return lax.dot_general(left, right, (((0,), (0,)), ((), ())), preferred_element_type=f32)


def pick_kernel(cells_hbm, plate_hbm, control_hbm, out_ref, cells, plate_ref, control_ref, sems, flag_sems):
    chunk = ROWS // 2
    flag_copies = [
        pltpu.make_async_copy(control_hbm, control_ref, flag_sems.at[0]),
        pltpu.make_async_copy(plate_hbm, plate_ref, flag_sems.at[1]),
    ]
    copies = [
        pltpu.make_async_copy(
            cells_hbm.at[pl.ds(part * chunk, chunk)], cells.at[pl.ds(part * chunk, chunk)], sems.at[part]
        )
        for part in range(2)
    ]
    for copy in flag_copies + copies:
        copy.start()
    group = lax.axis_index("d") // MEMBERS
    for copy in flag_copies:
        copy.wait()
    is_control = control_ref[...] == 1
    flags = is_control.astype(f32)
    upper = lax.broadcasted_iota(jnp.int32, (LANES, LANES), 0) <= lax.broadcasted_iota(
        jnp.int32, (LANES, LANES), 1
    )
    inclusive = matmul(flags.astype(bf16), upper.astype(f32).astype(bf16))
    total = jnp.broadcast_to(jnp.sum(flags, axis=1, keepdims=True), (SUBROWS, LANES))
    sub = lax.broadcasted_iota(jnp.int32, (SUBROWS, LANES), 0)
    running = total
    for step in (1, 2, 4):
        running = running + jnp.where(sub >= step, pltpu.roll(running, step, 0), 0.0)
    rank = jnp.where(is_control, inclusive + (running - total) - 1.0, -1.0).astype(jnp.int32)
    slots = lax.broadcasted_iota(jnp.int32, (BLOCK, LANES), 0)
    chosen = jnp.concatenate(
        [
            jnp.where(slots == jnp.broadcast_to(rank[k : k + 1, :], (BLOCK, LANES)), 1.0, 0.0).astype(bf16)
            for k in range(SUBROWS)
        ],
        axis=1,
    )
    earlier = jnp.sum(jnp.where(is_control & (plate_ref[...] < group), 1.0, 0.0), keepdims=True)
    picked = None
    for part, copy in enumerate(copies):
        copy.wait()
        span = slice(part * chunk, (part + 1) * chunk)
        term = matmul(chosen[:, span], cells[span, :])
        picked = term if picked is None else picked + term
    last = lax.broadcasted_iota(jnp.int32, (BLOCK, F), 0) == BLOCK - 1
    out_ref[...] = jnp.where(last, jnp.broadcast_to(earlier, (BLOCK, F)), picked).astype(bf16)


def sphere_kernel(rows_ref, group_ref, first_ref, out_ref, start_ref, rest_ref, raw_b, start_b, rest_b, left_b, iterate_b):
    index = lax.axis_index("d")
    group = index // MEMBERS
    home = (group + index) % 2
    last_home = (group == GROUPS - 1) & (home == 1)
    first_plate = group + home == 1
    slot = lax.broadcasted_iota(jnp.int32, (BLOCK, LANES), 0).astype(f32)
    blocks = []
    count = jnp.zeros((1, 1), f32)

    def keep(rows, low, high):
        flags = jnp.where((slot >= low) & (slot < high), 1.0, 0.0).astype(bf16)
        blocks.append(rows * jnp.concatenate([flags] * (F // LANES), axis=1))

    for block in range(6):
        earlier = rows_ref[(block + 1) * BLOCK - 16 : (block + 1) * BLOCK, 0:LANES].astype(f32)[15:16, 0:1]
        if block < 3:
            low, high = earlier, jnp.full((1, 1), float(CONTROLS), f32)
        else:
            low, high = jnp.zeros((1, 1), f32), jnp.where(last_home, 0.0, earlier)
        keep(rows_ref[block * BLOCK : (block + 1) * BLOCK, :], low, high)
        count = count + (high - low)
    opening = jnp.where(first_plate, float(CONTROLS), 0.0)
    keep(jnp.where(group == 0, group_ref[...], first_ref[...]), 0.0, opening)
    count = count + opening
    picked = jnp.concatenate(blocks, axis=0)
    scale = 1.0 / jnp.maximum(count, 1.0)
    centre_row = matmul(jnp.ones((16, 7 * BLOCK), bf16), picked)[0:1, :] * scale
    centre_column = jnp.broadcast_to(centre_row, (8, F)).T[:, 0:1]
    parts = [slice(0, HALF), slice(HALF, F)]
    quarters = [slice(k, k + LANES) for k in range(0, F, LANES)]
    eye = lax.broadcasted_iota(jnp.int32, (LANES, LANES), 0) == lax.broadcasted_iota(jnp.int32, (LANES, LANES), 1)
    squares = jnp.zeros((1, F), f32)
    for part in parts:
        covariance = matmul_tn(picked[:, part], picked) * scale - centre_column[part, :] * centre_row
        start_ref[part, :] = covariance
        raw_b[part, :] = covariance.astype(bf16)
        squares = squares + jnp.sum(covariance * covariance, axis=0, keepdims=True)
    traces = jnp.zeros((1, LANES), f32)
    for span in quarters:
        traces = traces + jnp.sum(jnp.where(eye, start_ref[span, span], 0.0), axis=0, keepdims=True)
    trace = jnp.sum(traces, keepdims=True)
    ridge = shrink * trace / F + epsilon
    keep_part = 1.0 - shrink
    norm_square = (
        keep_part * keep_part * jnp.sum(squares, keepdims=True) + 2.0 * keep_part * ridge * trace + F * ridge * ridge
    )
    norm_scale = jnp.sqrt(norm_square)
    slope = keep_part / norm_scale
    level = ridge / norm_scale
    for part in parts:
        products = matmul(raw_b[part, :], raw_b[...])
        for row in range(0, HALF, LANES):
            rows = slice(part.start + row, part.start + row + LANES)
            for columns in quarters:
                raw = start_ref[rows, columns]
                a = slope * raw
                square = (slope * slope) * products[row : row + LANES, columns] + (2.0 * slope * level) * raw
                if rows == columns:
                    a = a + jnp.where(eye, level, 0.0)
                    square = square + jnp.where(eye, level * level, 0.0)
                iterate = 1.5 * a - 0.5 * square
                start_ref[rows, columns] = a
                start_b[rows, columns] = a.astype(bf16)
                left_b[rows, columns] = (0.25 * square - 1.5 * a).astype(bf16)
                iterate_b[rows, columns] = iterate.astype(bf16)
                rest_ref[rows, columns] = -0.75 * a - 1.125 * iterate
    z = 2.25
    for step in range(2):
        for part in parts:
            rest = rest_ref[part, :] - 0.5 * matmul(left_b[part, :], iterate_b[...])
            rest_ref[part, :] = rest
            rest_b[part, :] = rest.astype(bf16)
        for part in parts:
            rest = rest_ref[part, :]
            both = matmul(jnp.concatenate([rest_b[part, :], start_b[part, :]], axis=0), rest_b[...])
            square = both[0:HALF, :]
            iterate = z * start_ref[part, :] + both[HALF:F, :]
            left_b[part, :] = (2.0 * z * rest + square).astype(bf16)
            iterate_b[part, :] = iterate.astype(bf16)
            rest_ref[part, :] = 1.5 * rest - (0.5 * z * z) * iterate
        z = 1.5 * z
    gain = lax.rsqrt(norm_scale)
    for span in quarters:
        rest_ref[span, span] = rest_ref[span, span] + jnp.where(eye, z, 0.0)
    upper, lower = parts
    sphere = (rest_ref[upper, :] - 0.5 * matmul(left_b[upper, :], iterate_b[...])) * gain
    out_ref[upper, :] = sphere.astype(bf16)
    corner = (rest_ref[lower, lower] - 0.5 * matmul(left_b[lower, :], iterate_b[:, lower])) * gain
    out_ref[HALF:CENTRE, 0:HALF] = corner[0 : HALF // 2, :].astype(bf16)
    out_ref[HALF:CENTRE, HALF:F] = corner[HALF // 2 : HALF, :].astype(bf16)
    out_ref[CENTRE:PACK, :] = jnp.broadcast_to(centre_row, (PACK - CENTRE, F)).astype(bf16)


def apply_kernel(cells_ref, plate_ref, packed_ref, out_hbm, out, spheres, sems):
    group = lax.axis_index("d") // MEMBERS
    parity = group % 2
    earlier = jnp.sum(jnp.where(plate_ref[...] < group, 1, 0))
    offsets = []
    for side, core in enumerate((parity, 1 - parity)):
        upper = packed_ref[core, 0:HALF, :]
        spheres[side, 0:HALF, :] = upper
        spheres[side, HALF:F, 0:HALF] = upper[:, HALF:F].T
        spheres[side, HALF:CENTRE, HALF:F] = packed_ref[core, HALF:CENTRE, 0:HALF]
        spheres[side, CENTRE:F, HALF:F] = packed_ref[core, HALF:CENTRE, HALF:F]
        offsets.append(matmul(packed_ref[core, CENTRE:PACK, :], spheres[side])[0:1, :])
    chunk = ROWS // CHUNKS
    mixed = jnp.minimum(earlier // chunk, CHUNKS - 1)
    rows = cells_ref[pl.ds(pl.multiple_of(mixed * chunk, chunk), chunk), :]
    own = matmul(rows, spheres[1]) - offsets[1]
    slot = lax.broadcasted_iota(jnp.int32, (chunk, F), 0)
    copies = []
    for part in range(CHUNKS):
        start = part * chunk
        span = slice(start, start + chunk)
        side = jnp.where(earlier > start, 0, 1)
        offset = jnp.where(earlier > start, offsets[0], offsets[1])
        values = matmul(cells_ref[span, :], spheres[side]) - offset
        limit = jnp.where(mixed == part, earlier - start, chunk)
        out[span, :] = jnp.where(slot < limit, values, own).astype(bf16)
        copy = pltpu.make_async_copy(out.at[pl.ds(start, chunk)], out_hbm.at[pl.ds(start, chunk)], sems.at[part])
        copy.start()
        copies.append(copy)
    for copy in copies:
        copy.wait()


def pairs(kind):
    if kind == "chip":
        return [[2 * i, 2 * i + 1] for i in range(GROUPS * MEMBERS // 2)]
    first = [MEMBERS * p + 1 - p % 2 for p in range(GROUPS)]
    near = [[d + 2, d + 4] for d in first[:-1]]
    far = [[d, d + 6] for d in first[:-1]]
    return near + far + [[0, 2], [first[-1], first[-1] + 2]]


def shards(cells, plate_id, control):
    vmem = pl.BlockSpec(memory_space=pltpu.VMEM)
    hbm = pl.BlockSpec(memory_space=pltpu.HBM)
    params = pltpu.CompilerParams(vmem_limit_bytes=VMEM_LIMIT)
    plates = plate_id.reshape(SUBROWS, LANES)
    block = pl.pallas_call(
        pick_kernel,
        out_shape=jax.ShapeDtypeStruct((BLOCK, F), bf16),
        in_specs=[hbm, hbm, hbm],
        out_specs=vmem,
        scratch_shapes=[
            pltpu.VMEM((ROWS, F), bf16),
            pltpu.VMEM((SUBROWS, LANES), jnp.int32),
            pltpu.VMEM((SUBROWS, LANES), jnp.int32),
            pltpu.SemaphoreType.DMA((2,)),
            pltpu.SemaphoreType.DMA((2,)),
        ],
        compiler_params=params,
        name="pick_controls",
    )(*(pltpu.with_memory_space_constraint(x, pltpu.HBM) for x in (cells, plates, control.reshape(SUBROWS, LANES))))
    members = [[MEMBERS * g + m for m in range(MEMBERS)] for g in range(GROUPS)]
    group_rows = lax.all_gather(block, "d", axis_index_groups=members, tiled=True)
    index = lax.axis_index("d")
    home = (index ^ (index >> 2)) & 1
    side = lax.dynamic_slice_in_dim(group_rows, home * BLOCK, HOME, 0)
    opening = group_rows[0:BLOCK]
    first = lax.ppermute(opening, "d", [(0, 5), (2, 7)])
    plate_rows = lax.all_gather(side, "d", axis_index_groups=pairs("plate"), tiled=True)
    sphere = pl.pallas_call(
        sphere_kernel,
        out_shape=jax.ShapeDtypeStruct((PACK, F), bf16),
        in_specs=[vmem, vmem, vmem],
        out_specs=vmem,
        scratch_shapes=[pltpu.VMEM((F, F), f32)] * 2 + [pltpu.VMEM((F, F), bf16)] * 5,
        compiler_params=params,
        name="sphere",
    )(plate_rows, opening, first)
    spheres = lax.all_gather(sphere, "d", axis_index_groups=pairs("chip"), tiled=True)
    return pl.pallas_call(
        apply_kernel,
        out_shape=jax.ShapeDtypeStruct((ROWS, F), bf16),
        in_specs=[vmem, vmem, vmem],
        out_specs=hbm,
        scratch_shapes=[
            pltpu.VMEM((ROWS, F), bf16),
            pltpu.VMEM((2, F, F), bf16),
            pltpu.SemaphoreType.DMA((CHUNKS,)),
        ],
        compiler_params=params,
        name="apply_spheres",
    )(cells, plates, spheres.reshape(2, PACK, F))


def solution(mesh):
    line = Mesh(mesh.devices.reshape(-1), ("d",))
    return jax.shard_map(
        shards,
        mesh=line,
        in_specs=(P("d", None), P("d"), P("d")),
        out_specs=P("d", None),
        check_vma=False,
    )
```

```python
import jax
import jax.numpy as jnp
from jax import lax
from jax.experimental import pallas as pl
from jax.experimental.pallas import tpu as pltpu
from jax.sharding import Mesh
from jax.sharding import PartitionSpec as P

ROWS = 1024
F = 512
CONTROLS = 93
BLOCK = 96
LANES = 128
SUBROWS = ROWS // LANES
MEMBERS = 4
CHUNKS = 8
HOME = 3 * BLOCK
GROUPS = 128
HALF = F // 2
CENTRE = HALF + HALF // 2
PACK = CENTRE + 16

shrink = 0.1
epsilon = 1e-05
f32 = jnp.float32
bf16 = jnp.bfloat16
VMEM_LIMIT = 48 * 1024 * 1024


def matmul(left, right):
    return jnp.dot(left, right, preferred_element_type=f32)


def matmul_tn(left, right):
    return lax.dot_general(left, right, (((0,), (0,)), ((), ())), preferred_element_type=f32)


def pick_kernel(cells_hbm, plate_hbm, control_hbm, out_ref, cells, plate_ref, control_ref, sems, flag_sems):
    chunk = ROWS // 2
    flag_copies = [
        pltpu.make_async_copy(control_hbm, control_ref, flag_sems.at[0]),
        pltpu.make_async_copy(plate_hbm, plate_ref, flag_sems.at[1]),
    ]
    copies = [
        pltpu.make_async_copy(
            cells_hbm.at[pl.ds(part * chunk, chunk)], cells.at[pl.ds(part * chunk, chunk)], sems.at[part]
        )
        for part in range(2)
    ]
    for copy in flag_copies + copies:
        copy.start()
    group = lax.axis_index("d") // MEMBERS
    for copy in flag_copies:
        copy.wait()
    is_control = control_ref[...] == 1
    flags = is_control.astype(f32)
    upper = lax.broadcasted_iota(jnp.int32, (LANES, LANES), 0) <= lax.broadcasted_iota(
        jnp.int32, (LANES, LANES), 1
    )
    inclusive = matmul(flags.astype(bf16), upper.astype(f32).astype(bf16))
    total = jnp.broadcast_to(jnp.sum(flags, axis=1, keepdims=True), (SUBROWS, LANES))
    sub = lax.broadcasted_iota(jnp.int32, (SUBROWS, LANES), 0)
    running = total
    for step in (1, 2, 4):
        running = running + jnp.where(sub >= step, pltpu.roll(running, step, 0), 0.0)
    rank = jnp.where(is_control, inclusive + (running - total) - 1.0, -1.0).astype(jnp.int32)
    slots = lax.broadcasted_iota(jnp.int32, (BLOCK, LANES), 0)
    chosen = jnp.concatenate(
        [
            jnp.where(slots == jnp.broadcast_to(rank[k : k + 1, :], (BLOCK, LANES)), 1.0, 0.0).astype(bf16)
            for k in range(SUBROWS)
        ],
        axis=1,
    )
    earlier = jnp.sum(jnp.where(is_control & (plate_ref[...] < group), 1.0, 0.0), keepdims=True)
    picked = None
    for part, copy in enumerate(copies):
        copy.wait()
        span = slice(part * chunk, (part + 1) * chunk)
        term = matmul(chosen[:, span], cells[span, :])
        picked = term if picked is None else picked + term
    last = lax.broadcasted_iota(jnp.int32, (BLOCK, F), 0) == BLOCK - 1
    out_ref[...] = jnp.where(last, jnp.broadcast_to(earlier, (BLOCK, F)), picked).astype(bf16)


def sphere_kernel(rows_ref, group_ref, first_ref, out_ref, start_ref, rest_ref, raw_b, start_b, rest_b, left_b, iterate_b):
    index = lax.axis_index("d")
    group = index // MEMBERS
    home = (index + index // 2) % 2
    last_home = (group == GROUPS - 1) & (home == 1)
    first_plate = group + home == 1
    slot = lax.broadcasted_iota(jnp.int32, (BLOCK, LANES), 0).astype(f32)
    blocks = []
    count = jnp.zeros((1, 1), f32)

    def keep(rows, low, high):
        flags = jnp.where((slot >= low) & (slot < high), 1.0, 0.0).astype(bf16)
        blocks.append(rows * jnp.concatenate([flags] * (F // LANES), axis=1))

    for block in range(6):
        earlier = rows_ref[(block + 1) * BLOCK - 16 : (block + 1) * BLOCK, 0:LANES].astype(f32)[15:16, 0:1]
        if block < 3:
            low, high = earlier, jnp.full((1, 1), float(CONTROLS), f32)
        else:
            low, high = jnp.zeros((1, 1), f32), jnp.where(last_home, 0.0, earlier)
        keep(rows_ref[block * BLOCK : (block + 1) * BLOCK, :], low, high)
        count = count + (high - low)
    opening = jnp.where(first_plate, float(CONTROLS), 0.0)
    keep(jnp.where(group == 0, group_ref[...], first_ref[...]), 0.0, opening)
    count = count + opening
    picked = jnp.concatenate(blocks, axis=0)
    scale = 1.0 / jnp.maximum(count, 1.0)
    centre_row = matmul(jnp.ones((16, 7 * BLOCK), bf16), picked)[0:1, :] * scale
    centre_column = jnp.broadcast_to(centre_row, (8, F)).T[:, 0:1]
    parts = [slice(0, HALF), slice(HALF, F)]
    quarters = [slice(k, k + LANES) for k in range(0, F, LANES)]
    eye = lax.broadcasted_iota(jnp.int32, (LANES, LANES), 0) == lax.broadcasted_iota(jnp.int32, (LANES, LANES), 1)
    squares = jnp.zeros((1, F), f32)
    for part in parts:
        covariance = matmul_tn(picked[:, part], picked) * scale - centre_column[part, :] * centre_row
        start_ref[part, :] = covariance
        raw_b[part, :] = covariance.astype(bf16)
        squares = squares + jnp.sum(covariance * covariance, axis=0, keepdims=True)
    traces = jnp.zeros((1, LANES), f32)
    for span in quarters:
        traces = traces + jnp.sum(jnp.where(eye, start_ref[span, span], 0.0), axis=0, keepdims=True)
    trace = jnp.sum(traces, keepdims=True)
    ridge = shrink * trace / F + epsilon
    keep_part = 1.0 - shrink
    norm_square = (
        keep_part * keep_part * jnp.sum(squares, keepdims=True) + 2.0 * keep_part * ridge * trace + F * ridge * ridge
    )
    norm_scale = jnp.sqrt(norm_square)
    slope = keep_part / norm_scale
    level = ridge / norm_scale
    for part in parts:
        products = matmul(raw_b[part, :], raw_b[...])
        for row in range(0, HALF, LANES):
            rows = slice(part.start + row, part.start + row + LANES)
            for columns in quarters:
                raw = start_ref[rows, columns]
                a = slope * raw
                square = (slope * slope) * products[row : row + LANES, columns] + (2.0 * slope * level) * raw
                if rows == columns:
                    a = a + jnp.where(eye, level, 0.0)
                    square = square + jnp.where(eye, level * level, 0.0)
                iterate = 1.5 * a - 0.5 * square
                start_ref[rows, columns] = a
                start_b[rows, columns] = a.astype(bf16)
                left_b[rows, columns] = (0.25 * square - 1.5 * a).astype(bf16)
                iterate_b[rows, columns] = iterate.astype(bf16)
                rest_ref[rows, columns] = -0.75 * a - 1.125 * iterate
    z = 2.25
    for step in range(2):
        for part in parts:
            rest = rest_ref[part, :] - 0.5 * matmul(left_b[part, :], iterate_b[...])
            rest_ref[part, :] = rest
            rest_b[part, :] = rest.astype(bf16)
        for part in parts:
            rest = rest_ref[part, :]
            both = matmul(jnp.concatenate([rest_b[part, :], start_b[part, :]], axis=0), rest_b[...])
            square = both[0:HALF, :]
            iterate = z * start_ref[part, :] + both[HALF:F, :]
            left_b[part, :] = (2.0 * z * rest + square).astype(bf16)
            iterate_b[part, :] = iterate.astype(bf16)
            rest_ref[part, :] = 1.5 * rest - (0.5 * z * z) * iterate
        z = 1.5 * z
    gain = lax.rsqrt(norm_scale)
    for span in quarters:
        rest_ref[span, span] = rest_ref[span, span] + jnp.where(eye, z, 0.0)
    upper, lower = parts
    sphere = (rest_ref[upper, :] - 0.5 * matmul(left_b[upper, :], iterate_b[...])) * gain
    out_ref[upper, :] = sphere.astype(bf16)
    corner = (rest_ref[lower, lower] - 0.5 * matmul(left_b[lower, :], iterate_b[:, lower])) * gain
    out_ref[HALF:CENTRE, 0:HALF] = corner[0 : HALF // 2, :].astype(bf16)
    out_ref[HALF:CENTRE, HALF:F] = corner[HALF // 2 : HALF, :].astype(bf16)
    out_ref[CENTRE:PACK, :] = jnp.broadcast_to(centre_row, (PACK - CENTRE, F)).astype(bf16)


def apply_kernel(cells_ref, plate_ref, packed_ref, out_hbm, out, spheres, sems):
    group = lax.axis_index("d") // MEMBERS
    parity = lax.axis_index("d") // 2 % 2
    earlier = jnp.sum(jnp.where(plate_ref[...] < group, 1, 0))
    offsets = []
    for side, core in enumerate((parity, 1 - parity)):
        upper = packed_ref[core, 0:HALF, :]
        spheres[side, 0:HALF, :] = upper
        spheres[side, HALF:F, 0:HALF] = upper[:, HALF:F].T
        spheres[side, HALF:CENTRE, HALF:F] = packed_ref[core, HALF:CENTRE, 0:HALF]
        spheres[side, CENTRE:F, HALF:F] = packed_ref[core, HALF:CENTRE, HALF:F]
        offsets.append(matmul(packed_ref[core, CENTRE:PACK, :], spheres[side])[0:1, :])
    chunk = ROWS // CHUNKS
    mixed = jnp.minimum(earlier // chunk, CHUNKS - 1)
    rows = cells_ref[pl.ds(pl.multiple_of(mixed * chunk, chunk), chunk), :]
    own = matmul(rows, spheres[1]) - offsets[1]
    slot = lax.broadcasted_iota(jnp.int32, (chunk, F), 0)
    copies = []
    for part in range(CHUNKS):
        start = part * chunk
        span = slice(start, start + chunk)
        side = jnp.where(earlier > start, 0, 1)
        offset = jnp.where(earlier > start, offsets[0], offsets[1])
        values = matmul(cells_ref[span, :], spheres[side]) - offset
        limit = jnp.where(mixed == part, earlier - start, chunk)
        out[span, :] = jnp.where(slot < limit, values, own).astype(bf16)
        copy = pltpu.make_async_copy(out.at[pl.ds(start, chunk)], out_hbm.at[pl.ds(start, chunk)], sems.at[part])
        copy.start()
        copies.append(copy)
    for copy in copies:
        copy.wait()


def pairs(kind):
    if kind == "chip":
        return [[2 * i, 2 * i + 1] for i in range(GROUPS * MEMBERS // 2)]
    near = [[4 * p + 2, 4 * p + 4] for p in range(GROUPS - 1)]
    far = [[4 * p + 1, 4 * p + 7] for p in range(GROUPS - 1)]
    return near + far + [[0, 3], [4 * GROUPS - 3, 4 * GROUPS - 2]]


def shards(cells, plate_id, control):
    vmem = pl.BlockSpec(memory_space=pltpu.VMEM)
    hbm = pl.BlockSpec(memory_space=pltpu.HBM)
    params = pltpu.CompilerParams(vmem_limit_bytes=VMEM_LIMIT)
    plates = plate_id.reshape(SUBROWS, LANES)
    block = pl.pallas_call(
        pick_kernel,
        out_shape=jax.ShapeDtypeStruct((BLOCK, F), bf16),
        in_specs=[hbm, hbm, hbm],
        out_specs=vmem,
        scratch_shapes=[
            pltpu.VMEM((ROWS, F), bf16),
            pltpu.VMEM((SUBROWS, LANES), jnp.int32),
            pltpu.VMEM((SUBROWS, LANES), jnp.int32),
            pltpu.SemaphoreType.DMA((2,)),
            pltpu.SemaphoreType.DMA((2,)),
        ],
        compiler_params=params,
        name="pick_controls",
    )(*(pltpu.with_memory_space_constraint(x, pltpu.HBM) for x in (cells, plates, control.reshape(SUBROWS, LANES))))
    members = [[MEMBERS * g + m for m in range(MEMBERS)] for g in range(GROUPS)]
    group_rows = lax.all_gather(block, "d", axis_index_groups=members, tiled=True)
    index = lax.axis_index("d")
    home = (index ^ (index >> 1)) & 1
    side = lax.dynamic_slice_in_dim(group_rows, home * BLOCK, HOME, 0)
    opening = group_rows[0:BLOCK]
    first = lax.ppermute(opening, "d", [(0, 4), (2, 7)])
    plate_rows = lax.all_gather(side, "d", axis_index_groups=pairs("plate"), tiled=True)
    sphere = pl.pallas_call(
        sphere_kernel,
        out_shape=jax.ShapeDtypeStruct((PACK, F), bf16),
        in_specs=[vmem, vmem, vmem],
        out_specs=vmem,
        scratch_shapes=[pltpu.VMEM((F, F), f32)] * 2 + [pltpu.VMEM((F, F), bf16)] * 5,
        compiler_params=params,
        name="sphere",
    )(plate_rows, opening, first)
    spheres = lax.all_gather(sphere, "d", axis_index_groups=pairs("chip"), tiled=True)
    return pl.pallas_call(
        apply_kernel,
        out_shape=jax.ShapeDtypeStruct((ROWS, F), bf16),
        in_specs=[vmem, vmem, vmem],
        out_specs=hbm,
        scratch_shapes=[
            pltpu.VMEM((ROWS, F), bf16),
            pltpu.VMEM((2, F, F), bf16),
            pltpu.SemaphoreType.DMA((CHUNKS,)),
        ],
        compiler_params=params,
        name="apply_spheres",
    )(cells, plates, spheres.reshape(2, PACK, F))


def solution(mesh):
    line = Mesh(mesh.devices.reshape(-1), ("d",))
    return jax.shard_map(
        shards,
        mesh=line,
        in_specs=(P("d", None), P("d"), P("d")),
        out_specs=P("d", None),
        check_vma=False,
    )
```
